32 devices in a mesh: strike: 8 (over z, y), dip: 4 (over x, core).
Axes of the slice: x: 2, y: 2, z: 4, core: 2. Of those that a mesh axis runs over, the one named last changes fastest.
Arguments:
- slip: float32 [4096, 2048], P('strike', 'dip'), may hold values from 0 to 2
- rate: float32 [4096, 2048], P('strike', 'dip'), may hold values from 0 to 2
- prestress: float32 [4096, 2048], P('strike', 'dip'), may hold values from 0 to 1.5
- normal_stress: float32 [4096, 2048], P('strike', 'dip'), may hold values from 0.5 to 1.5
- history: float32 [8, 2, 4096, 2048], P(None, None, 'strike', 'dip'), may hold values from -6 to 6
- fric_flag: int32 [4096, 2048], P('strike', 'dip'), may hold values 0 or 1
- row_dest: int32 [4, 32768, 1], P('dip', 'strike'), may hold values from 0 to 7; in each aligned block of 4096 rows (0 to 4095, 4096 to 8191, ..., all dimensions but the last counted through in order) at most 1024 rows name the same one
- row_node: int32 [4, 32768], P('dip', 'strike'), may hold values from 0 to 262143
- fe_traction: float32 [4, 32768], P('dip', 'strike'), may hold values from -8 to 8
- fe_count: int32 [4, 8], P('dip', 'strike'), may hold values from 1 to 4096, 24576 in all within a row
Outputs:
- new_rate: float32 [4096, 2048], P('strike', 'dip')
- stress: float32 [4096, 2048], P('strike', 'dip')
- fe_rate: float32 [4, 32768], P('dip', 'strike')
The draws below stay inside these ranges and needn't reach their ends.
Inputs may be any that keep to these rules, and one draw needn't show every extreme that they name: `row_dest`: among the 4096 rows of one partition at most 1024 name the same strike block, and some partition has exactly 1024 rows naming one block. `fe_count`: the counts of one dip row sum to 3 * 4096 * P // 4 with P the number of strike devices; some partition is full.
All inputs are finite; a program needn't handle non-finite values. No bound on the sum of `fric_flag` on one device may be relied on, other than what follows from the above.
Results may differ from the reference program's by a relative error of at most 0.0003.
Values sent between devices are 32-bit elements; how exact they have to be, the bound alone decides.
A program may use at most 128 MiB of HBM per device.

```python
import math
import jax
import jax.numpy as jnp
import numpy as np
from jax import lax

NS = 4096
ND = 2048
LAGS = 8
ROWS = 4096
CAP = 1024
N_STRIKE = 8
N_DIP = 4


def with_ends(drawn, key, low, largest):
    index_at = [jax.random.randint(jax.random.fold_in(key, axis), (), 0, length) for axis, length in enumerate(drawn.shape)]
    longest = drawn.shape.index(max(drawn.shape))
    beside = index_at[:longest] + [(index_at[longest] + 1) % drawn.shape[longest]] + index_at[longest + 1:]
    return drawn.at[tuple(index_at)].set(low).at[tuple(beside)].set(largest)


def steps_of(own_key, shape, split, low, top_value):
    loudness = 1.0
    for axis_at, parts in split:
        draws = jax.random.uniform(jax.random.fold_in(jax.random.fold_in(own_key, 6), axis_at), (parts,), jnp.float32, low / len(split), top_value / len(split))
        loudness = loudness * jnp.repeat(jnp.exp(draws), shape[axis_at] // parts).reshape((-1,) + (1,) * (len(shape) - 1 - axis_at))
    return loudness


def split_up(count, total, most, skew):
    loads = [(1 << 20) // math.isqrt(rank ** skew) + 1 for rank in range(2, count + 1)]
    surplus, counts = total - most - (count - 1), [1] * (count - 1)
    while surplus > 0:
        free = [i for i in range(count - 1) if counts[i] < most]
        mass, budget = sum([loads[i] for i in free]), surplus
        for i in free:
            extra = min(most - counts[i], max(1, budget * loads[i] // mass), surplus)
            counts[i] = counts[i] + extra
            surplus = surplus - extra
    return np.array([most] + counts)


def uneven_parts(rng, number_of, total, bound, slope):
    if number_of == 2:
        one = jax.random.randint(rng, (), max(1, total - bound), min(bound, total - 1) + 1)
        return jnp.stack([one, total - one])
    lengths = jnp.asarray(split_up(number_of, total, bound, slope), jnp.int32)
    twos = (number_of - 1) // 2
    source_of, receiver = lengths[1:1 + 2 * twos:2], lengths[2:2 + 2 * twos:2]
    room = jnp.minimum(source_of - 1, bound - receiver)
    shifted = jax.random.randint(jax.random.fold_in(rng, 1), (twos,), 0, 1 << 20) % (room + 1)
    lengths = lengths.at[1:1 + 2 * twos:2].set(source_of - shifted).at[2:2 + 2 * twos:2].set(receiver + shifted)
    return lengths[jax.random.permutation(jax.random.fold_in(rng, 2), number_of)]


def routed_block(stream_key, own, number, rows, number_of, top, bound, lean):
    sequence = jax.random.permutation(stream_key, number_of)
    crowded, usual = shares(number_of, rows * top, bound, lean, True), shares(number_of, rows * top, bound, lean, False)
    places = jnp.arange(number_of)

    def named(sizes, rotation):
        used = int((sizes > 0).sum())
        fixed = max(1, used // 4)
        moved = fixed + (places - fixed + rotation * (used - fixed)) % max(1, number_of - fixed)
        return jnp.zeros((number_of,), jnp.int32).at[sequence[jnp.where(places < fixed, places, moved)]].set(jnp.asarray(sizes, jnp.int32))

    sizes = jnp.where(number % 4 == 0, named(crowded, number // 4), named(usual, number - number // 4 - 1))
    mixed = jax.random.permutation(jax.random.fold_in(own, 3), number_of)
    giver, sink = mixed[0:number_of // 2 * 2:2], mixed[1:number_of // 2 * 2:2]
    slack = jnp.minimum(sizes[giver] - 1, bound - sizes[sink]) // 2
    slack = jnp.where((giver == sequence[0]) | (sink == sequence[0]) | (sizes[sink] == 0), 0, jnp.maximum(slack, 0))
    moved = jax.random.randint(jax.random.fold_in(own, 4), (number_of // 2,), 0, 1 << 20) % (slack + 1)
    sizes = sizes.at[giver].add(-moved).at[sink].add(moved)
    labels = jnp.searchsorted(jnp.cumsum(sizes), jnp.arange(rows * top), side="right").astype(jnp.int32)
    grid = labels.reshape(top, rows).T
    grid = grid[jax.random.permutation(jax.random.fold_in(own, 1), rows)]
    rotation = jax.random.randint(jax.random.fold_in(own, 2), (rows, 1), 0, top)
    return jnp.take_along_axis(grid, (jnp.arange(top)[None, :] + rotation) % top, axis=1)


def shares(amount, total, most, slope, full):
    loads = [(1 << 20) // math.isqrt(rank ** slope) + 1 for rank in range(1, amount + 1)]
    largest = most if full else min(most, max(-(-total // amount), total * loads[0] // sum(loads)))
    least = 1 if total - largest >= amount - 1 else 0
    given, rest = [largest] + [least] * (amount - 1), total - largest - least * (amount - 1)
    while rest > 0:
        free = [i for i in range(1, amount) if given[i] < largest] or [i for i in range(1, amount) if given[i] < most]
        mass, left = sum([loads[i] for i in free]), rest
        for i in free:
            addition = min(most - given[i], max(1, left * loads[i] // mass), rest)
            given[i] = given[i] + addition
            rest = rest - addition
    return np.array(given)


def noise(own_key, dims, width, most, shards=(), kind=jnp.bfloat16):
    values = jax.random.normal(own_key, dims, jnp.float32) * width
    if len(shards) > 0:
        values = steps_of(own_key, dims, shards, -0.22, 0.18) * values
    return jnp.clip(values, min=-most, max=most).astype(kind)


def setup_inputs(seed: int = 0) -> dict:
    key_list = jax.random.split(jax.random.key(seed), 11)
    slip = jnp.clip(2.0 * jax.random.uniform(key_list[0], (NS, ND), jnp.float32) ** steps_of(key_list[0], (NS, ND), ((0, 8), (1, 4)), -0.2, 0.2), 0.0, 2.0)
    rate = jnp.clip(2.0 * jax.random.uniform(key_list[1], (NS, ND), jnp.float32) ** steps_of(key_list[1], (NS, ND), ((0, 8), (1, 4)), -0.2, 0.2), 0.0, 2.0)
    prestress = jnp.clip(1.5 * jax.random.uniform(key_list[2], (NS, ND), jnp.float32) ** steps_of(key_list[2], (NS, ND), ((0, 8), (1, 4)), -0.2, 0.2), 0.0, 1.5)
    normal_stress = jnp.clip(0.5 + 1.0 * jax.random.uniform(key_list[3], (NS, ND), jnp.float32) ** steps_of(key_list[3], (NS, ND), ((0, 8), (1, 4)), -0.2, 0.2), 0.5, 1.5)
    history = noise(key_list[4], (LAGS, 2, NS, ND), 1.0, 6.0, ((2, 8), (3, 4)), jnp.float32)
    fric_flag = with_ends((jax.random.randint(key_list[5], (NS, ND), 0, 4) < 3).astype(jnp.int32), jax.random.fold_in(key_list[5], 1), 0, 1)
    row_dest_keys = jax.random.split(jax.random.fold_in(key_list[6], 1), N_DIP * (N_STRIKE * ROWS) // ROWS)
    row_dest_turns = jax.random.permutation(jax.random.fold_in(key_list[6], 3), N_DIP * (N_STRIKE * ROWS) // ROWS)
    row_dest = jax.vmap(lambda own, number: routed_block(jax.random.fold_in(key_list[6], 2), own, number, ROWS, N_STRIKE, 1, CAP, 2))(row_dest_keys, row_dest_turns).reshape((N_DIP, N_STRIKE * ROWS, 1))
    row_node = with_ends(jax.random.randint(key_list[7], (N_DIP, N_STRIKE * ROWS), 0, NS * ND // (N_STRIKE * N_DIP)), jax.random.fold_in(key_list[7], 1), 0, (NS * ND // (N_STRIKE * N_DIP)) - 1).astype(jnp.int32)
    fe_traction = noise(key_list[8], (N_DIP, N_STRIKE * ROWS), 2.0, 8.0, ((0, 4), (1, 8)), jnp.float32)
    fe_count = jax.vmap(lambda own: uneven_parts(own, N_STRIKE, 3 * ROWS * N_STRIKE // 4, ROWS, 2))(jax.random.split(key_list[9], N_DIP)).reshape((N_DIP, N_STRIKE)).astype(jnp.int32)
    return dict(slip=slip, rate=rate, prestress=prestress, normal_stress=normal_stress, history=history, fric_flag=fric_flag, row_dest=row_dest, row_node=row_node, fe_traction=fe_traction, fe_count=fe_count)


full_turn = 2.0 * math.pi
STEP_DT = 0.5
SHEAR_MOD = 1.0
DAMPING = 0.5
STATIC_FR = 0.6
DYNAMIC_FR = 0.4
KERNEL_DT = 0.5
KERNEL_DECAY = 0.15
KERNEL_FREQ = 0.9

def reverse_bits(indices, levels):
    result = indices * 0
    for bit_index in range(levels):
        result = result + indices // 2 ** bit_index % 2 * 2 ** (levels - 1 - bit_index)
    return result

def wavenumber(freq_row, freq_col, length_row, length_col):
    signed_row = jnp.where(freq_row >= length_row // 2, freq_row - length_row, freq_row).astype(jnp.float32) / length_row
    signed_col = jnp.where(freq_col >= length_col // 2, freq_col - length_col, freq_col).astype(jnp.float32) / length_col
    return full_turn * jnp.sqrt(signed_row * signed_row + signed_col * signed_col)

def memory_sum(history, wavenum):
    real_part = jnp.zeros_like(wavenum)
    imag_part = jnp.zeros_like(wavenum)
    for lag_index in range(history.shape[0]):
        spacing = (lag_index + 1) * wavenum
        weight = KERNEL_DT * jnp.exp(-KERNEL_DECAY * spacing) * jnp.cos(KERNEL_FREQ * spacing)
        real_part = real_part + weight * history[lag_index, 0]
        imag_part = imag_part + weight * history[lag_index, 1]
    return (real_part, imag_part)

def reference(slip, rate, prestress, normal_stress, history, fric_flag, row_dest, row_node, fe_traction, fe_count):
    levels = N_STRIKE.bit_length() - 1
    rows_dev = NS // N_STRIKE
    cols_dev = ND // N_DIP
    scaling = 1.0 / math.sqrt(NS * ND)
    slip_new = slip + STEP_DT * rate
    position = jnp.arange(NS, dtype=jnp.int32)
    freq_of = reverse_bits(position // rows_dev, levels) + N_STRIKE * (position % rows_dev)
    spot_of = reverse_bits(position % N_STRIKE, levels) * rows_dev + position // N_STRIKE
    natural = jnp.fft.fft2(slip_new) * scaling
    spectrum = natural[freq_of]
    freq_row = jnp.broadcast_to(freq_of[:, None], (NS, ND))
    freq_col = jnp.broadcast_to(jnp.arange(ND, dtype=jnp.int32)[None, :], (NS, ND))
    wavenum = wavenumber(freq_row, freq_col, NS, ND)
    memory_re, memory_im = memory_sum(history, wavenum)
    factor = -0.5 * SHEAR_MOD * wavenum
    func_spec = lax.complex(factor * (jnp.real(spectrum) - memory_re), factor * (jnp.imag(spectrum) - memory_im))
    functional = jnp.real(jnp.fft.ifft2(func_spec[spot_of])) * (NS * ND) * scaling
    target = row_dest[:, :, 0]
    row_pos = jnp.arange(N_STRIKE * ROWS, dtype=jnp.int32)
    active = (row_pos % ROWS)[None, :] < jnp.repeat(fe_count, ROWS, axis=1)
    strike_at = target * rows_dev + row_node // cols_dev
    dip_at = jnp.arange(N_DIP, dtype=jnp.int32)[:, None] * cols_dev + row_node % cols_dev
    traction = jnp.zeros((NS, ND), jnp.float32).at[strike_at, dip_at].add(jnp.where(active, fe_traction, 0.0))
    stress = prestress + functional + traction
    strength = normal_stress * (STATIC_FR - (STATIC_FR - DYNAMIC_FR) * jnp.minimum(slip_new, 1.0))
    new_rate = jnp.where(fric_flag == 1, jnp.maximum(stress - strength, 0.0) / DAMPING, 0.0)
    fe_rate = jnp.where(active, new_rate[strike_at, dip_at], 0.0)
    return (new_rate, stress, fe_rate)
```

```python
import math

import jax
import jax.numpy as jnp
import numpy as np
from jax import lax
from jax.sharding import PartitionSpec as P

full_turn = 2.0 * math.pi
high = lax.Precision.HIGH
highest = lax.Precision.HIGHEST
STEP_DT = 0.5
SHEAR_MOD = 1.0
DAMPING = 0.5
STATIC_FR = 0.6
DYNAMIC_FR = 0.4
KERNEL_DT = 0.5
KERNEL_DECAY = 0.15
KERNEL_FREQ = 0.9


def reverse_bits(indices, levels):
    result = indices * 0
    for bit_index in range(levels):
        result = result + indices // 2**bit_index % 2 * 2 ** (levels - 1 - bit_index)
    return result


def wavenumber(freq_row, freq_col, length_row, length_col):
    signed_row = (
        jnp.where(freq_row >= length_row // 2, freq_row - length_row, freq_row).astype(jnp.float32)
        / length_row
    )
    signed_col = (
        jnp.where(freq_col >= length_col // 2, freq_col - length_col, freq_col).astype(jnp.float32)
        / length_col
    )
    return full_turn * jnp.sqrt(signed_row * signed_row + signed_col * signed_col)


def memory_sum(history, wavenum):
    decay = jnp.exp(-KERNEL_DECAY * wavenum)
    base_re = decay * jnp.cos(KERNEL_FREQ * wavenum)
    base_im = decay * jnp.sin(KERNEL_FREQ * wavenum)
    power_re, power_im = base_re, base_im
    real_part = power_re * history[0, 0]
    imag_part = power_re * history[0, 1]
    for lag_index in range(1, history.shape[0]):
        power_re, power_im = (
            power_re * base_re - power_im * base_im,
            power_re * base_im + power_im * base_re,
        )
        real_part = real_part + power_re * history[lag_index, 0]
        imag_part = imag_part + power_re * history[lag_index, 1]
    return (KERNEL_DT * real_part, KERNEL_DT * imag_part)


def dip_table(blocks, groups, total_dip):
    half = total_dip // 2
    per_dip = half // groups
    per_device = per_dip // blocks
    strike_at = np.arange(blocks)[:, None, None]
    dip_at = np.arange(groups)[None, :, None]
    turn = np.where(dip_at < groups // 2, 2 * dip_at, 2 * (groups - 1 - dip_at) + 1)
    modes = turn * per_dip + strike_at * per_device + np.arange(per_device)[None, None, :]
    modes = modes.reshape(blocks * groups, per_device)
    place = np.arange(total_dip)
    angle = (modes[:, :, None] * place % total_dip) * (full_turn / total_dip)
    cos_part = np.cos(angle)
    sin_part = -np.sin(angle)
    sin_part = np.where(modes[:, :, None] == 0, 1.0 - 2.0 * (place % 2), sin_part)
    table = np.stack([cos_part, sin_part], axis=1)
    return table.reshape(2 * half, total_dip).astype(np.float32)


def line_table(length, sign):
    angle = (np.outer(np.arange(length), np.arange(length)) % length) * (full_turn / length)
    cos_part, sin_part = np.cos(angle), sign * np.sin(angle)
    return np.block([[cos_part, sin_part], [-sin_part, cos_part]]).astype(np.float32)


def twiddles(blocks, length):
    angle = np.outer(np.arange(blocks), np.arange(length)) * (full_turn / (blocks * length))
    return np.cos(angle).astype(np.float32), np.sin(angle).astype(np.float32)


def short_transform(parts, sign):
    count = len(parts)
    if count == 1:
        return parts
    even = short_transform(parts[0::2], sign)
    odd = short_transform(parts[1::2], sign)
    first, second = [], []
    for index in range(count // 2):
        even_re, even_im = even[index]
        odd_re, odd_im = odd[index]
        if index == 0:
            turned_re, turned_im = odd_re, odd_im
        elif 4 * index == count:
            turned_re, turned_im = -sign * odd_im, sign * odd_re
        else:
            cos_part = math.cos(full_turn * index / count)
            sin_part = sign * math.sin(full_turn * index / count)
            turned_re = odd_re * cos_part - odd_im * sin_part
            turned_im = odd_re * sin_part + odd_im * cos_part
        first.append((even_re + turned_re, even_im + turned_im))
        second.append((even_re - turned_re, even_im - turned_im))
    return first + second


def block_transform(real_part, imag_part, sign):
    blocks = real_part.shape[1]
    if blocks <= 16:
        parts = [(real_part[:, j], imag_part[:, j]) for j in range(blocks)]
        parts = short_transform(parts, sign)
        return (
            jnp.stack([part[0] for part in parts], axis=1),
            jnp.stack([part[1] for part in parts], axis=1),
        )
    table = line_table(blocks, sign).reshape(2, blocks, 2, blocks)
    out = jnp.einsum(
        "pkjm,pjqr->qkrm", jnp.stack([real_part, imag_part]), table, precision=high
    )
    return out[0], out[1]


def slot_ranks(target, blocks):
    count_rows = target.shape[0]
    block_len = math.gcd(count_rows, 512)
    onehot = (target[:, None] == lax.broadcasted_iota(jnp.int32, (1, blocks), 1)).astype(
        jnp.float32
    )
    onehot = onehot.reshape(count_rows // block_len, block_len, blocks)
    triangle = (
        lax.broadcasted_iota(jnp.int32, (block_len, block_len), 0)
        >= lax.broadcasted_iota(jnp.int32, (block_len, block_len), 1)
    ).astype(jnp.float32)
    running = jnp.einsum("ij,bjk->bik", triangle, onehot)
    totals = jnp.sum(onehot, axis=1)
    before = jnp.cumsum(totals, axis=0) - totals
    running = running + before[:, None, :]
    slot_rank = jnp.sum(running * onehot, axis=2) - 1.0
    return slot_rank.reshape(count_rows).astype(jnp.int32)


def pick(indices, count):
    return (indices[:, None] == lax.broadcasted_iota(jnp.int32, (1, count), 1)).astype(jnp.float32)


def body(
    slip,
    rate,
    prestress,
    normal_stress,
    history,
    fric_flag,
    row_dest,
    row_node,
    fe_traction,
    fe_count,
):
    blocks = lax.axis_size("strike")
    groups = lax.axis_size("dip")
    levels = blocks.bit_length() - 1
    strike_pos = lax.axis_index("strike")
    dip_pos = lax.axis_index("dip")
    rows_here = slip.shape[0]
    cols_here = slip.shape[1]
    total_strike = rows_here * blocks
    total_dip = cols_here * groups
    scaling = 1.0 / math.sqrt(total_strike * total_dip)
    devices = blocks * groups
    half_cols = cols_here // 2
    per_device = half_cols // blocks
    rows_line = rows_here // groups
    both = ("strike", "dip")
    rev = [int(v) for v in reverse_bits(np.arange(blocks), levels)]

    target = row_dest[0, :, 0]
    node_ids = row_node[0]
    count_rows = target.shape[0]
    capacity = 2 * count_rows // blocks
    active = lax.broadcasted_iota(jnp.int32, (count_rows,), 0) < fe_count[0, 0]
    slot_ids = target * capacity + slot_ranks(target, blocks)
    lanes = 128
    slot_high = pick(slot_ids // lanes, blocks * capacity // lanes)
    slot_low = pick(slot_ids % lanes, lanes)
    payload = jnp.stack([jnp.where(active, fe_traction[0], 0.0), node_ids.astype(jnp.float32)])
    outbox = jnp.einsum("pi,ia,ib->pab", payload, slot_high, slot_low, precision=highest)
    received = lax.all_to_all(
        outbox.reshape(2, blocks, capacity), "strike", split_axis=1, concat_axis=1, tiled=True
    )
    flat_nodes = (received[1].reshape(-1) + 0.5).astype(jnp.int32)
    pick_row = pick(flat_nodes // cols_here, rows_here)
    pick_col = pick(flat_nodes % cols_here, cols_here)
    traction = jnp.einsum(
        "ir,ic->rc", pick_row * received[0].reshape(-1)[:, None], pick_col, precision=high
    )

    slip_new = slip + STEP_DT * rate
    wave_table = jnp.asarray(dip_table(blocks, groups, total_dip))
    lines = lax.all_to_all(slip_new, "dip", split_axis=0, concat_axis=1, tiled=True)
    modes = jnp.einsum("kc,rc->kr", wave_table, lines, precision=high)
    modes = modes.reshape(devices, 2 * per_device, rows_line)
    modes = lax.all_to_all(modes, both, split_axis=0, concat_axis=0, tiled=True)
    modes = jnp.swapaxes(modes, 0, 1).reshape(2, per_device, blocks, rows_here)
    line_re = jnp.concatenate([modes[0], modes[0, :1]], axis=0)
    line_im = jnp.concatenate([modes[1], -modes[1, :1]], axis=0)
    line_re, line_im = block_transform(line_re, line_im, -1.0)
    turn_cos, turn_sin = twiddles(blocks, rows_here)
    line_re, line_im = (
        line_re * turn_cos + line_im * turn_sin,
        line_im * turn_cos - line_re * turn_sin,
    )
    spec = jnp.concatenate([line_re, line_im], axis=-1)
    spec = jnp.einsum("krm,mq->krq", spec, line_table(rows_here, -1.0), precision=high)

    turn_at = jnp.where(dip_pos < groups // 2, 2 * dip_pos, 2 * (groups - 1 - dip_pos) + 1)
    first_mode = turn_at * half_cols + strike_pos * per_device
    dims = (per_device, blocks, rows_here)
    mode_at = first_mode + lax.broadcasted_iota(jnp.int32, dims, 0)
    freq_row = lax.broadcasted_iota(jnp.int32, dims, 1) + blocks * lax.broadcasted_iota(
        jnp.int32, dims, 2
    )
    factor = -0.5 * SHEAR_MOD * scaling * scaling
    filt = 2.0 * factor * wavenumber(freq_row, mode_at, total_strike, total_dip)
    filt = jnp.concatenate([filt, filt], axis=-1)
    is_first = first_mode == 0
    edge_row = freq_row[:1]
    edge_low = factor * wavenumber(edge_row, edge_row * 0, total_strike, total_dip)
    edge_top = factor * wavenumber(
        edge_row, edge_row * 0 + total_dip // 2, total_strike, total_dip
    )
    edge_low = jnp.concatenate([edge_low, edge_low], axis=-1)
    edge_top = jnp.concatenate([edge_top, edge_top], axis=-1)
    direct, mirror = spec[:1], spec[per_device:]
    edge = 0.5 * (edge_low * (direct + mirror) + edge_top * (direct - mirror))
    spec = spec[:per_device] * filt
    spec = jnp.concatenate([jnp.where(is_first, edge, spec[:1]), spec[1:]], axis=0)
    spec = jnp.einsum("krq,qm->krm", spec, line_table(rows_here, 1.0), precision=high)
    back_re, back_im = spec[..., :rows_here], spec[..., rows_here:]
    back_re, back_im = (
        back_re * turn_cos - back_im * turn_sin,
        back_im * turn_cos + back_re * turn_sin,
    )

    residue = reverse_bits(strike_pos, levels)
    dims = (rows_here, cols_here)
    freq_row = residue + blocks * lax.broadcasted_iota(jnp.int32, dims, 0)
    freq_col = dip_pos * cols_here + lax.broadcasted_iota(jnp.int32, dims, 1)
    wavenum = wavenumber(freq_row, freq_col, total_strike, total_dip)
    memory_re, memory_im = memory_sum(history, wavenum)
    gain = (0.5 * SHEAR_MOD * scaling) * wavenum
    memory = jnp.concatenate([gain * memory_re, gain * memory_im], axis=0)
    memory = jnp.einsum("qk,qm->km", memory, line_table(rows_here, 1.0), precision=high)
    here_cos = lax.dynamic_slice_in_dim(jnp.asarray(turn_cos), residue, 1, 0)
    here_sin = lax.dynamic_slice_in_dim(jnp.asarray(turn_sin), residue, 1, 0)
    mem_re, mem_im = memory[:, :rows_here], memory[:, rows_here:]
    memory = jnp.concatenate(
        [mem_re * here_cos - mem_im * here_sin, mem_im * here_cos + mem_re * here_sin], axis=1
    )
    upper = list(range(groups // 2, groups))
    edge_moves = [(upper[(i + 1) % len(upper)], upper[i]) for i in range(len(upper))]
    edge_mode = lax.ppermute(memory[:1], "dip", edge_moves)
    mirrored = jnp.concatenate([edge_mode, jnp.flip(memory[1:], axis=0)], axis=0)
    memory = jnp.where(dip_pos < groups // 2, memory, mirrored)
    lower_side = dip_pos < groups // 2
    keep = jnp.where(lower_side, memory[:half_cols], memory[half_cols:])
    give = jnp.where(lower_side, memory[half_cols:], memory[:half_cols])
    given = lax.ppermute(give, "dip", [(i, groups - 1 - i) for i in range(groups)])
    straight = jnp.where(lower_side, keep, given)
    mirrored = jnp.where(lower_side, given, keep)
    memory = jnp.stack([straight, mirrored]).reshape(2, blocks, per_device, 2 * rows_here)
    memory = lax.all_to_all(memory, "strike", split_axis=1, concat_axis=1, tiled=True)
    straight_re = [memory[0, rev[r], :, :rows_here] for r in range(blocks)]
    straight_im = [memory[0, rev[r], :, rows_here:] for r in range(blocks)]
    mirror_re = [memory[1, rev[r], :, :rows_here] for r in range(blocks)]
    mirror_im = [memory[1, rev[r], :, rows_here:] for r in range(blocks)]
    slot_first = (lax.broadcasted_iota(jnp.int32, (per_device, 1), 0) == 0) & is_first
    folded_re, folded_im = [], []
    for r in range(blocks):
        o = (blocks - r) % blocks
        edge_re = 0.5 * (straight_re[r] + straight_re[o] - mirror_im[r] + mirror_im[o])
        edge_im = 0.5 * (straight_im[r] - straight_im[o] + mirror_re[r] + mirror_re[o])
        folded_re.append(jnp.where(slot_first, edge_re, straight_re[r] + mirror_re[o]))
        folded_im.append(jnp.where(slot_first, edge_im, straight_im[r] - mirror_im[o]))
    back_re = back_re + jnp.stack(folded_re, axis=1)
    back_im = back_im + jnp.stack(folded_im, axis=1)

    back_re, back_im = block_transform(back_re, back_im, 1.0)
    back = jnp.stack([back_re, back_im]).reshape(2 * per_device, devices, rows_line)
    back = lax.all_to_all(
        jnp.swapaxes(back, 0, 1), both, split_axis=0, concat_axis=0, tiled=True
    )
    back = back.reshape(total_dip, rows_line)
    functional = jnp.einsum("kr,kc->rc", back, wave_table, precision=high)
    functional = lax.all_to_all(functional, "dip", split_axis=1, concat_axis=0, tiled=True)

    stress = prestress + functional + traction
    strength = normal_stress * (STATIC_FR - (STATIC_FR - DYNAMIC_FR) * jnp.minimum(slip_new, 1.0))
    new_rate = jnp.where(fric_flag == 1, jnp.maximum(stress - strength, 0.0) / DAMPING, 0.0)
    sampled = jnp.einsum("ir,rc->ic", pick_row, new_rate, precision=high)
    sampled = jnp.sum(sampled * pick_col, axis=1).reshape(blocks, capacity)
    returned = lax.all_to_all(sampled, "strike", split_axis=0, concat_axis=0, tiled=True)
    returned = jnp.einsum(
        "ia,ab->ib", slot_high, returned.reshape(-1, lanes), precision=highest
    )
    fe_rate = jnp.where(active, jnp.sum(returned * slot_low, axis=1), 0.0)
    return (new_rate, stress, fe_rate[None])


def solution(mesh):
    in_specs = (
        P("strike", "dip"),
        P("strike", "dip"),
        P("strike", "dip"),
        P("strike", "dip"),
        P(None, None, "strike", "dip"),
        P("strike", "dip"),
        P("dip", "strike", None),
        P("dip", "strike"),
        P("dip", "strike"),
        P("dip", "strike"),
    )
    out_specs = (P("strike", "dip"), P("strike", "dip"), P("dip", "strike"))
    return jax.shard_map(body, mesh=mesh, in_specs=in_specs, out_specs=out_specs, check_vma=False)
```

```python
import math

import jax
import jax.numpy as jnp
import numpy as np
from jax import lax
from jax.sharding import PartitionSpec as P

full_turn = 2.0 * math.pi
high = lax.Precision.HIGH
highest = lax.Precision.HIGHEST
STEP_DT = 0.5
SHEAR_MOD = 1.0
DAMPING = 0.5
STATIC_FR = 0.6
DYNAMIC_FR = 0.4
KERNEL_DT = 0.5
KERNEL_DECAY = 0.15
KERNEL_FREQ = 0.9


def reverse_bits(indices, levels):
    result = indices * 0
    for bit_index in range(levels):
        result = result + indices // 2**bit_index % 2 * 2 ** (levels - 1 - bit_index)
    return result


def wavenumber(freq_row, freq_col, length_row, length_col):
    signed_row = (
        jnp.where(freq_row >= length_row // 2, freq_row - length_row, freq_row).astype(jnp.float32)
        / length_row
    )
    signed_col = (
        jnp.where(freq_col >= length_col // 2, freq_col - length_col, freq_col).astype(jnp.float32)
        / length_col
    )
    return full_turn * jnp.sqrt(signed_row * signed_row + signed_col * signed_col)


def memory_sum(history, wavenum):
    decay = jnp.exp(-KERNEL_DECAY * wavenum)
    base_re = decay * jnp.cos(KERNEL_FREQ * wavenum)
    base_im = decay * jnp.sin(KERNEL_FREQ * wavenum)
    power_re, power_im = base_re, base_im
    real_part = power_re * history[0, 0]
    imag_part = power_re * history[0, 1]
    for lag_index in range(1, history.shape[0]):
        power_re, power_im = (
            power_re * base_re - power_im * base_im,
            power_re * base_im + power_im * base_re,
        )
        real_part = real_part + power_re * history[lag_index, 0]
        imag_part = imag_part + power_re * history[lag_index, 1]
    return (KERNEL_DT * real_part, KERNEL_DT * imag_part)


def dip_table(blocks, groups, total_dip):
    half = total_dip // 2
    per_dip = half // groups
    per_device = per_dip // blocks
    strike_at = np.arange(blocks)[:, None, None]
    dip_at = np.arange(groups)[None, :, None]
    turn = np.where(dip_at < groups // 2, 2 * dip_at, 2 * (groups - 1 - dip_at) + 1)
    modes = turn * per_dip + strike_at * per_device + np.arange(per_device)[None, None, :]
    modes = modes.reshape(blocks * groups, per_device)
    place = np.arange(total_dip)
    angle = (modes[:, :, None] * place % total_dip) * (full_turn / total_dip)
    cos_part = np.cos(angle)
    sin_part = -np.sin(angle)
    sin_part = np.where(modes[:, :, None] == 0, 1.0 - 2.0 * (place % 2), sin_part)
    table = np.stack([cos_part, sin_part], axis=1)
    return table.reshape(2 * half, total_dip).astype(np.float32)


def line_table(length, sign):
    angle = (np.outer(np.arange(length), np.arange(length)) % length) * (full_turn / length)
    cos_part, sin_part = np.cos(angle), sign * np.sin(angle)
    return np.block([[cos_part, sin_part], [-sin_part, cos_part]]).astype(np.float32)


def twiddles(blocks, length):
    angle = np.outer(np.arange(blocks), np.arange(length)) * (full_turn / (blocks * length))
    return np.cos(angle).astype(np.float32), np.sin(angle).astype(np.float32)


def short_transform(parts, sign):
    count = len(parts)
    if count == 1:
        return parts
    even = short_transform(parts[0::2], sign)
    odd = short_transform(parts[1::2], sign)
    first, second = [], []
    for index in range(count // 2):
        even_re, even_im = even[index]
        odd_re, odd_im = odd[index]
        if index == 0:
            turned_re, turned_im = odd_re, odd_im
        elif 4 * index == count:
            turned_re, turned_im = -sign * odd_im, sign * odd_re
        else:
            cos_part = math.cos(full_turn * index / count)
            sin_part = sign * math.sin(full_turn * index / count)
            turned_re = odd_re * cos_part - odd_im * sin_part
            turned_im = odd_re * sin_part + odd_im * cos_part
        first.append((even_re + turned_re, even_im + turned_im))
        second.append((even_re - turned_re, even_im - turned_im))
    return first + second


def block_transform(real_part, imag_part, sign):
    blocks = real_part.shape[1]
    if blocks <= 16:
        parts = [(real_part[:, j], imag_part[:, j]) for j in range(blocks)]
        parts = short_transform(parts, sign)
        return (
            jnp.stack([part[0] for part in parts], axis=1),
            jnp.stack([part[1] for part in parts], axis=1),
        )
    table = line_table(blocks, sign).reshape(2, blocks, 2, blocks)
    out = jnp.einsum(
        "pkjm,pjqr->qkrm", jnp.stack([real_part, imag_part]), table, precision=high
    )
    return out[0], out[1]


def halves(values):
    upper = lax.reduce_precision(values, 8, 7)
    return upper.astype(jnp.bfloat16), (values - upper).astype(jnp.bfloat16)


def table_halves(table):
    upper = table.astype(jnp.bfloat16)
    lower = (table - upper.astype(np.float32)).astype(jnp.bfloat16)
    return jnp.asarray(upper), jnp.asarray(lower)


def dot_f32(pattern, left, right):
    return jnp.einsum(pattern, left, right, preferred_element_type=jnp.float32)


def slot_ranks(target, blocks):
    count_rows = target.shape[0]
    block_len = math.gcd(count_rows, 512)
    onehot = (target[:, None] == lax.broadcasted_iota(jnp.int32, (1, blocks), 1)).astype(
        jnp.float32
    )
    onehot = onehot.reshape(count_rows // block_len, block_len, blocks)
    triangle = (
        lax.broadcasted_iota(jnp.int32, (block_len, block_len), 0)
        >= lax.broadcasted_iota(jnp.int32, (block_len, block_len), 1)
    ).astype(jnp.float32)
    running = jnp.einsum("ij,bjk->bik", triangle, onehot)
    totals = jnp.sum(onehot, axis=1)
    before = jnp.cumsum(totals, axis=0) - totals
    running = running + before[:, None, :]
    slot_rank = jnp.sum(running * onehot, axis=2) - 1.0
    return slot_rank.reshape(count_rows).astype(jnp.int32)


def pick(indices, count):
    return (indices[:, None] == lax.broadcasted_iota(jnp.int32, (1, count), 1)).astype(jnp.float32)


def body(
    slip,
    rate,
    prestress,
    normal_stress,
    history,
    fric_flag,
    row_dest,
    row_node,
    fe_traction,
    fe_count,
):
    blocks = lax.axis_size("strike")
    groups = lax.axis_size("dip")
    levels = blocks.bit_length() - 1
    strike_pos = lax.axis_index("strike")
    dip_pos = lax.axis_index("dip")
    rows_here = slip.shape[0]
    cols_here = slip.shape[1]
    total_strike = rows_here * blocks
    total_dip = cols_here * groups
    scaling = 1.0 / math.sqrt(total_strike * total_dip)
    devices = blocks * groups
    half_cols = cols_here // 2
    per_device = half_cols // blocks
    rows_line = rows_here // groups
    both = ("strike", "dip")
    rev = [int(v) for v in reverse_bits(np.arange(blocks), levels)]

    target = row_dest[0, :, 0]
    node_ids = row_node[0]
    count_rows = target.shape[0]
    capacity = 2 * count_rows // blocks
    active = lax.broadcasted_iota(jnp.int32, (count_rows,), 0) < fe_count[0, 0]
    slot_ids = target * capacity + slot_ranks(target, blocks)
    lanes = 128
    slot_high = pick(slot_ids // lanes, blocks * capacity // lanes)
    slot_low = pick(slot_ids % lanes, lanes)
    payload = jnp.stack([jnp.where(active, fe_traction[0], 0.0), node_ids.astype(jnp.float32)])
    outbox = jnp.einsum("pi,ia,ib->pab", payload, slot_high, slot_low, precision=highest)
    received = lax.all_to_all(
        outbox.reshape(2, blocks, capacity), "strike", split_axis=1, concat_axis=1, tiled=True
    )
    slip_new = slip + STEP_DT * rate
    wave_upper, wave_lower = table_halves(dip_table(blocks, groups, total_dip))
    lines = lax.all_to_all(slip_new, "dip", split_axis=0, concat_axis=1, tiled=True)

    residue = reverse_bits(strike_pos, levels)
    dims = (rows_here, cols_here)
    freq_row = residue + blocks * lax.broadcasted_iota(jnp.int32, dims, 0)
    freq_col = dip_pos * cols_here + lax.broadcasted_iota(jnp.int32, dims, 1)
    wavenum = wavenumber(freq_row, freq_col, total_strike, total_dip)
    memory_re, memory_im = memory_sum(history, wavenum)
    gain = (0.5 * SHEAR_MOD * scaling) * wavenum
    memory = jnp.concatenate([gain * memory_re, gain * memory_im], axis=0)
    lines, received, memory = lax.optimization_barrier((lines, received, memory))

    lines_upper, lines_lower = halves(lines)
    modes = dot_f32("kc,rc->kr", wave_upper, jnp.concatenate([lines_upper, lines_lower], axis=0))
    modes = modes[:, :rows_line] + modes[:, rows_line:]
    modes = modes + dot_f32("kc,rc->kr", wave_lower, lines_upper)
    modes = modes.reshape(devices, 2 * per_device, rows_line)
    modes = lax.all_to_all(modes, both, split_axis=0, concat_axis=0, tiled=True)

    flat_nodes = (received[1].reshape(-1) + 0.5).astype(jnp.int32)
    pick_row = pick(flat_nodes // cols_here, rows_here)
    pick_col = pick(flat_nodes % cols_here, cols_here)
    traction = jnp.einsum(
        "ir,ic->rc", pick_row * received[0].reshape(-1)[:, None], pick_col, precision=high
    )

    turn_cos, turn_sin = twiddles(blocks, rows_here)
    memory = jnp.einsum("qk,qm->km", memory, line_table(rows_here, 1.0), precision=high)
    here_cos = lax.dynamic_slice_in_dim(jnp.asarray(turn_cos), residue, 1, 0)
    here_sin = lax.dynamic_slice_in_dim(jnp.asarray(turn_sin), residue, 1, 0)
    mem_re, mem_im = memory[:, :rows_here], memory[:, rows_here:]
    memory = jnp.concatenate(
        [mem_re * here_cos - mem_im * here_sin, mem_im * here_cos + mem_re * here_sin], axis=1
    )
    sign = jnp.where(lax.broadcasted_iota(jnp.int32, (1, 2 * rows_here), 1) < rows_here, 1.0, -1.0)
    opposite = [rev[(blocks - rev[s]) % blocks] for s in range(blocks)]
    lower_side = dip_pos < groups // 2
    first_row = memory[:1]
    other = lax.ppermute(
        first_row,
        both,
        [(s * groups + d, opposite[s] * groups + d) for s in range(blocks) for d in range(groups)],
    )
    own_mirror = (dip_pos == 0) | (dip_pos == groups // 2)
    first_row = jnp.where(own_mirror, 0.5 * (first_row + sign * other), first_row)
    upper = list(range(groups // 2, groups))
    edge_moves = [(upper[(i + 1) % len(upper)], upper[i]) for i in range(len(upper))]
    edge_row = lax.ppermute(first_row, "dip", edge_moves)
    first_row = jnp.where(lower_side, first_row, edge_row)
    place = lax.broadcasted_iota(jnp.int32, (cols_here, cols_here), 0)
    place = jnp.where(lower_side, place, (cols_here - place) % cols_here)
    turned = (place == lax.broadcasted_iota(jnp.int32, (cols_here, cols_here), 1)).astype(
        jnp.bfloat16
    )
    mem_upper, mem_lower = halves(memory)
    memory = dot_f32("ak,km->am", turned, jnp.concatenate([mem_upper, mem_lower], axis=1))
    memory = memory[:, : 2 * rows_here] + memory[:, 2 * rows_here :]
    at_first = lax.broadcasted_iota(jnp.int32, (cols_here, 1), 0) == 0
    memory = jnp.where(at_first, first_row, memory)
    keep = jnp.where(lower_side, memory[:half_cols], memory[half_cols:])
    give = jnp.where(lower_side, memory[half_cols:], memory[:half_cols])
    given = lax.ppermute(
        give,
        both,
        [
            (s * groups + d, opposite[s] * groups + groups - 1 - d)
            for s in range(blocks)
            for d in range(groups)
        ],
    )
    folded = jnp.where(lower_side, keep, given) + sign * jnp.where(lower_side, given, keep)
    packed = jnp.concatenate(
        [keep[:1, :rows_here] + given[:1, rows_here:], keep[:1, rows_here:] + given[:1, :rows_here]],
        axis=1,
    )
    at_first = lax.broadcasted_iota(jnp.int32, (half_cols, 1), 0) == 0
    folded = jnp.where(at_first & (dip_pos == 0), packed, folded)
    modes, folded = lax.optimization_barrier((modes, folded))
    folded = folded.reshape(blocks, per_device, 2 * rows_here)
    folded = lax.all_to_all(folded, "strike", split_axis=0, concat_axis=0, tiled=True)

    modes = jnp.swapaxes(modes, 0, 1).reshape(2, per_device, blocks, rows_here)
    line_re = jnp.concatenate([modes[0], modes[0, :1]], axis=0)
    line_im = jnp.concatenate([modes[1], -modes[1, :1]], axis=0)
    line_re, line_im = block_transform(line_re, line_im, -1.0)
    line_re, line_im = (
        line_re * turn_cos + line_im * turn_sin,
        line_im * turn_cos - line_re * turn_sin,
    )
    spec = jnp.concatenate([line_re, line_im], axis=-1)
    spec = jnp.einsum("krm,mq->krq", spec, line_table(rows_here, -1.0), precision=high)

    turn_at = jnp.where(dip_pos < groups // 2, 2 * dip_pos, 2 * (groups - 1 - dip_pos) + 1)
    first_mode = turn_at * half_cols + strike_pos * per_device
    dims = (per_device, blocks, rows_here)
    mode_at = first_mode + lax.broadcasted_iota(jnp.int32, dims, 0)
    freq_row = lax.broadcasted_iota(jnp.int32, dims, 1) + blocks * lax.broadcasted_iota(
        jnp.int32, dims, 2
    )
    factor = -0.5 * SHEAR_MOD * scaling * scaling
    filt = 2.0 * factor * wavenumber(freq_row, mode_at, total_strike, total_dip)
    filt = jnp.concatenate([filt, filt], axis=-1)
    is_first = first_mode == 0
    edge_row = freq_row[:1]
    edge_low = factor * wavenumber(edge_row, edge_row * 0, total_strike, total_dip)
    edge_top = factor * wavenumber(
        edge_row, edge_row * 0 + total_dip // 2, total_strike, total_dip
    )
    edge_low = jnp.concatenate([edge_low, edge_low], axis=-1)
    edge_top = jnp.concatenate([edge_top, edge_top], axis=-1)
    direct, mirror = spec[:1], spec[per_device:]
    edge = 0.5 * (edge_low * (direct + mirror) + edge_top * (direct - mirror))
    spec = spec[:per_device] * filt
    spec = jnp.concatenate([jnp.where(is_first, edge, spec[:1]), spec[1:]], axis=0)
    spec = jnp.einsum("krq,qm->krm", spec, line_table(rows_here, 1.0), precision=high)
    back_re, back_im = spec[..., :rows_here], spec[..., rows_here:]
    back_re, back_im = (
        back_re * turn_cos - back_im * turn_sin,
        back_im * turn_cos + back_re * turn_sin,
    )

    back_re, back_im, folded, traction = lax.optimization_barrier(
        (back_re, back_im, folded, traction)
    )
    parts = []
    for r in range(blocks):
        o = (blocks - r) % blocks
        parts.append(jnp.where(lower_side, folded[rev[r]], folded[rev[o]]))
    back_re = back_re + jnp.stack([part[:, :rows_here] for part in parts], axis=1)
    back_im = back_im + jnp.stack([part[:, rows_here:] for part in parts], axis=1)

    back_re, back_im = block_transform(back_re, back_im, 1.0)
    back = jnp.stack([back_re, back_im]).reshape(2 * per_device, devices, rows_line)
    back = lax.all_to_all(
        jnp.swapaxes(back, 0, 1), both, split_axis=0, concat_axis=0, tiled=True
    )
    back = back.reshape(total_dip, rows_line)
    back_upper, back_lower = halves(back)
    functional = dot_f32("kr,kc->rc", jnp.concatenate([back_upper, back_lower], axis=1), wave_upper)
    functional = functional[:rows_line] + functional[rows_line:]
    functional = functional + dot_f32("kr,kc->rc", back_upper, wave_lower)
    functional = lax.all_to_all(functional, "dip", split_axis=1, concat_axis=0, tiled=True)

    stress = prestress + functional + traction
    strength = normal_stress * (STATIC_FR - (STATIC_FR - DYNAMIC_FR) * jnp.minimum(slip_new, 1.0))
    new_rate = jnp.where(fric_flag == 1, jnp.maximum(stress - strength, 0.0) / DAMPING, 0.0)
    sampled = jnp.einsum("ir,rc->ic", pick_row, new_rate, precision=high)
    sampled = jnp.sum(sampled * pick_col, axis=1).reshape(blocks, capacity)
    returned = lax.all_to_all(sampled, "strike", split_axis=0, concat_axis=0, tiled=True)
    returned = jnp.einsum(
        "ia,ab->ib", slot_high, returned.reshape(-1, lanes), precision=highest
    )
    fe_rate = jnp.where(active, jnp.sum(returned * slot_low, axis=1), 0.0)
    return (new_rate, stress, fe_rate[None])


def solution(mesh):
    in_specs = (
        P("strike", "dip"),
        P("strike", "dip"),
        P("strike", "dip"),
        P("strike", "dip"),
        P(None, None, "strike", "dip"),
        P("strike", "dip"),
        P("dip", "strike", None),
        P("dip", "strike"),
        P("dip", "strike"),
        P("dip", "strike"),
    )
    out_specs = (P("strike", "dip"), P("strike", "dip"), P("dip", "strike"))
    return jax.shard_map(body, mesh=mesh, in_specs=in_specs, out_specs=out_specs, check_vma=False)
```

```python
import functools
import math

import jax
import jax.numpy as jnp
import numpy as np
from jax import lax
from jax.experimental import pallas as pl
from jax.experimental.pallas import tpu as pltpu
from jax.sharding import PartitionSpec as P

full_turn = 2.0 * math.pi
high = lax.Precision.HIGH
highest = lax.Precision.HIGHEST
STEP_DT = 0.5
SHEAR_MOD = 1.0
DAMPING = 0.5
STATIC_FR = 0.6
DYNAMIC_FR = 0.4
KERNEL_DT = 0.5
KERNEL_DECAY = 0.15
KERNEL_FREQ = 0.9


def reverse_bits(indices, levels):
    result = indices * 0
    for bit_index in range(levels):
        result = result + indices // 2**bit_index % 2 * 2 ** (levels - 1 - bit_index)
    return result


def wavenumber(freq_row, freq_col, length_row, length_col):
    signed_row = (
        jnp.where(freq_row >= length_row // 2, freq_row - length_row, freq_row).astype(jnp.float32)
        / length_row
    )
    signed_col = (
        jnp.where(freq_col >= length_col // 2, freq_col - length_col, freq_col).astype(jnp.float32)
        / length_col
    )
    return full_turn * jnp.sqrt(signed_row * signed_row + signed_col * signed_col)


def cos_sin(angle):
    t = 0.5 * angle - 1.0
    t2 = t * t
    cos_t = 1.0 + t2 * (
        -1 / 2 + t2 * (1 / 24 + t2 * (-1 / 720 + t2 * (1 / 40320 - t2 * (1 / 3628800))))
    )
    sin_t = t * (
        1.0 + t2 * (-1 / 6 + t2 * (1 / 120 + t2 * (-1 / 5040 + t2 * (1 / 362880))))
    )
    cos_half = math.cos(1.0) * cos_t - math.sin(1.0) * sin_t
    sin_half = math.sin(1.0) * cos_t + math.cos(1.0) * sin_t
    return 1.0 - 2.0 * sin_half * sin_half, 2.0 * sin_half * cos_half


def memory_kernel(blocks, total_strike, total_dip, gain, place_ref, history_ref, out_ref):
    rows, cols = out_ref.shape[1:]
    row_at = pl.program_id(0) * rows + lax.broadcasted_iota(jnp.int32, (rows, cols), 0)
    freq_row = place_ref[0] + blocks * row_at
    freq_col = place_ref[1] + lax.broadcasted_iota(jnp.int32, (rows, cols), 1)
    wavenum = wavenumber(freq_row, freq_col, total_strike, total_dip)
    decay = jnp.exp(-KERNEL_DECAY * wavenum)
    cos_part, sin_part = cos_sin(KERNEL_FREQ * wavenum)
    base_re, base_im = decay * cos_part, decay * sin_part
    power_re, power_im = base_re, base_im
    real_part = power_re * history_ref[0, 0]
    imag_part = power_re * history_ref[0, 1]
    for lag_index in range(1, history_ref.shape[0]):
        power_re, power_im = (
            power_re * base_re - power_im * base_im,
            power_re * base_im + power_im * base_re,
        )
        real_part = real_part + power_re * history_ref[lag_index, 0]
        imag_part = imag_part + power_re * history_ref[lag_index, 1]
    scale = (gain * KERNEL_DT) * wavenum
    out_ref[0] = scale * real_part
    out_ref[1] = scale * imag_part


def weighted_history(history, place, blocks, total_strike, total_dip, gain):
    lags, _, rows, cols = history.shape
    tile = math.gcd(rows, 64)
    return pl.pallas_call(
        functools.partial(memory_kernel, blocks, total_strike, total_dip, gain),
        grid=(rows // tile,),
        out_shape=jax.ShapeDtypeStruct((2, rows, cols), jnp.float32),
        in_specs=[
            pl.BlockSpec(memory_space=pltpu.SMEM),
            pl.BlockSpec((lags, 2, tile, cols), lambda i: (0, 0, i, 0)),
        ],
        out_specs=pl.BlockSpec((2, tile, cols), lambda i: (0, i, 0)),
        compiler_params=pltpu.CompilerParams(vmem_limit_bytes=32 * 2**20),
        cost_estimate=pl.CostEstimate(
            flops=100 * rows * cols, bytes_accessed=4 * history.size, transcendentals=0
        ),
        name="weighted_history",
    )(place, history)


def dip_table(blocks, groups, total_dip):
    half = total_dip // 2
    per_dip = half // groups
    per_device = per_dip // blocks
    strike_at = np.arange(blocks)[:, None, None]
    dip_at = np.arange(groups)[None, :, None]
    turn = np.where(dip_at < groups // 2, 2 * dip_at, 2 * (groups - 1 - dip_at) + 1)
    modes = turn * per_dip + strike_at * per_device + np.arange(per_device)[None, None, :]
    modes = modes.reshape(blocks * groups, per_device)
    place = np.arange(total_dip)
    angle = (modes[:, :, None] * place % total_dip) * (full_turn / total_dip)
    cos_part = np.cos(angle)
    sin_part = -np.sin(angle)
    sin_part = np.where(modes[:, :, None] == 0, 1.0 - 2.0 * (place % 2), sin_part)
    table = np.stack([cos_part, sin_part], axis=1)
    return table.reshape(2 * half, total_dip).astype(np.float32)


def line_table(length, sign):
    angle = (np.outer(np.arange(length), np.arange(length)) % length) * (full_turn / length)
    cos_part, sin_part = np.cos(angle), sign * np.sin(angle)
    return np.block([[cos_part, sin_part], [-sin_part, cos_part]]).astype(np.float32)


def twiddles(blocks, length):
    angle = np.outer(np.arange(blocks), np.arange(length)) * (full_turn / (blocks * length))
    return np.cos(angle).astype(np.float32), np.sin(angle).astype(np.float32)


def short_transform(parts, sign):
    count = len(parts)
    if count == 1:
        return parts
    even = short_transform(parts[0::2], sign)
    odd = short_transform(parts[1::2], sign)
    first, second = [], []
    for index in range(count // 2):
        even_re, even_im = even[index]
        odd_re, odd_im = odd[index]
        if index == 0:
            turned_re, turned_im = odd_re, odd_im
        elif 4 * index == count:
            turned_re, turned_im = -sign * odd_im, sign * odd_re
        else:
            cos_part = math.cos(full_turn * index / count)
            sin_part = sign * math.sin(full_turn * index / count)
            turned_re = odd_re * cos_part - odd_im * sin_part
            turned_im = odd_re * sin_part + odd_im * cos_part
        first.append((even_re + turned_re, even_im + turned_im))
        second.append((even_re - turned_re, even_im - turned_im))
    return first + second


def block_transform(real_part, imag_part, sign):
    blocks = real_part.shape[1]
    if blocks <= 16:
        parts = [(real_part[:, j], imag_part[:, j]) for j in range(blocks)]
        parts = short_transform(parts, sign)
        return (
            jnp.stack([part[0] for part in parts], axis=1),
            jnp.stack([part[1] for part in parts], axis=1),
        )
    table = line_table(blocks, sign).reshape(2, blocks, 2, blocks)
    out = jnp.einsum(
        "pkjm,pjqr->qkrm", jnp.stack([real_part, imag_part]), table, precision=high
    )
    return out[0], out[1]


def halves(values):
    upper = lax.reduce_precision(values, 8, 7)
    return upper.astype(jnp.bfloat16), (values - upper).astype(jnp.bfloat16)


def table_halves(table):
    upper = table.astype(jnp.bfloat16)
    lower = (table - upper.astype(np.float32)).astype(jnp.bfloat16)
    return jnp.asarray(upper), jnp.asarray(lower)


def dot_f32(pattern, left, right):
    return jnp.einsum(pattern, left, right, preferred_element_type=jnp.float32)


def slot_ranks(target, active, blocks):
    count_rows = target.shape[0]
    block_len = math.gcd(count_rows, 512)
    named = jnp.where(active, target, blocks)
    onehot = pick(named, blocks)
    onehot = onehot.reshape(count_rows // block_len, block_len, blocks)
    triangle = (
        lax.broadcasted_iota(jnp.int32, (block_len, block_len), 0)
        >= lax.broadcasted_iota(jnp.int32, (block_len, block_len), 1)
    ).astype(jnp.float32)
    running = jnp.einsum("ij,bjk->bik", triangle, onehot)
    totals = jnp.sum(onehot, axis=1)
    before = jnp.cumsum(totals, axis=0) - totals
    running = running + before[:, None, :]
    slot_rank = jnp.sum(running * onehot, axis=2) - 1.0
    return slot_rank.reshape(count_rows).astype(jnp.int32)


def pick(indices, count):
    return (indices[:, None] == lax.broadcasted_iota(jnp.int32, (1, count), 1)).astype(jnp.float32)


def node_masks(node_ref, chunk, rows, cols):
    node = node_ref[chunk].astype(jnp.int32) - 1
    slots = node.shape[1]
    row_at, col_at = lax.shift_right_arithmetic(node, cols.bit_length() - 1), node & (cols - 1)
    in_row = lax.broadcasted_iota(jnp.int32, (rows, slots), 0) == row_at
    in_col = lax.broadcasted_iota(jnp.int32, (cols, slots), 0) == col_at
    return in_row, in_col


def split_in_kernel(values):
    upper = values.astype(jnp.bfloat16)
    return upper, (values - upper.astype(jnp.float32)).astype(jnp.bfloat16)


def scatter_kernel(used_ref, node_ref, value_ref, out_ref):
    rows, cols = out_ref.shape
    out_ref[...] = jnp.zeros_like(out_ref)

    def step(chunk, carry):
        @pl.when(used_ref[chunk] > 0)
        def _():
            in_row, in_col = node_masks(node_ref, chunk, rows, cols)
            spread = jnp.where(in_row, value_ref[chunk], 0.0)
            upper, lower = split_in_kernel(spread)
            ones = in_col.astype(jnp.float32).astype(jnp.bfloat16)
            dims = (((1,), (1,)), ((), ()))
            out_ref[...] += lax.dot_general(
                upper, ones, dims, preferred_element_type=jnp.float32
            ) + lax.dot_general(lower, ones, dims, preferred_element_type=jnp.float32)

        return carry

    lax.fori_loop(0, node_ref.shape[0], step, 0)


def gather_kernel(used_ref, node_ref, grid_ref, out_ref, upper_ref, lower_ref):
    rows, cols = grid_ref.shape
    upper_ref[...], lower_ref[...] = split_in_kernel(grid_ref[...])

    def step(chunk, carry):
        out_ref[chunk] = jnp.zeros(out_ref.shape[1:], jnp.float32)

        @pl.when(used_ref[chunk] > 0)
        def _():
            in_row, in_col = node_masks(node_ref, chunk, rows, cols)
            ones = in_col.astype(jnp.float32).astype(jnp.bfloat16)
            lines = jnp.dot(upper_ref[...], ones, preferred_element_type=jnp.float32) + jnp.dot(
                lower_ref[...], ones, preferred_element_type=jnp.float32
            )
            out_ref[chunk] = jnp.sum(jnp.where(in_row, lines, 0.0), axis=0, keepdims=True)

        return carry

    lax.fori_loop(0, node_ref.shape[0], step, 0)


in_vmem = pl.BlockSpec(memory_space=pltpu.VMEM)
in_smem = pl.BlockSpec(memory_space=pltpu.SMEM)
vmem_limit = 48 * 2**20


def scatter_rows(used, nodes, values, rows, cols):
    return pl.pallas_call(
        scatter_kernel,
        out_shape=jax.ShapeDtypeStruct((rows, cols), jnp.float32),
        in_specs=[in_smem, in_vmem, in_vmem],
        out_specs=in_vmem,
        compiler_params=pltpu.CompilerParams(vmem_limit_bytes=vmem_limit),
        cost_estimate=pl.CostEstimate(
            flops=2 * nodes.size * rows * cols, bytes_accessed=4 * rows * cols, transcendentals=0
        ),
        name="scatter_rows",
    )(used, nodes, values)


def gather_rows(used, nodes, grid):
    rows, cols = grid.shape
    return pl.pallas_call(
        gather_kernel,
        out_shape=jax.ShapeDtypeStruct(nodes.shape, jnp.float32),
        in_specs=[in_smem, in_vmem, in_vmem],
        out_specs=in_vmem,
        scratch_shapes=[pltpu.VMEM((rows, cols), jnp.bfloat16)] * 2,
        compiler_params=pltpu.CompilerParams(vmem_limit_bytes=vmem_limit),
        cost_estimate=pl.CostEstimate(
            flops=2 * nodes.size * rows * cols, bytes_accessed=4 * rows * cols, transcendentals=0
        ),
        name="gather_rows",
    )(used, nodes, grid)


def body(
    slip,
    rate,
    prestress,
    normal_stress,
    history,
    fric_flag,
    row_dest,
    row_node,
    fe_traction,
    fe_count,
):
    blocks = lax.axis_size("strike")
    groups = lax.axis_size("dip")
    levels = blocks.bit_length() - 1
    strike_pos = lax.axis_index("strike")
    dip_pos = lax.axis_index("dip")
    rows_here = slip.shape[0]
    cols_here = slip.shape[1]
    total_strike = rows_here * blocks
    total_dip = cols_here * groups
    scaling = 1.0 / math.sqrt(total_strike * total_dip)
    devices = blocks * groups
    half_cols = cols_here // 2
    per_device = half_cols // blocks
    rows_line = rows_here // groups
    both = ("strike", "dip")
    rev = [int(v) for v in reverse_bits(np.arange(blocks), levels)]

    target = row_dest[0, :, 0]
    node_ids = row_node[0]
    count_rows = target.shape[0]
    capacity = 2 * count_rows // blocks
    active = lax.broadcasted_iota(jnp.int32, (count_rows,), 0) < fe_count[0, 0]
    slot_ids = target * capacity + slot_ranks(target, active, blocks)
    slot_ids = jnp.where(active, slot_ids, -1)
    lanes = 128
    slot_high = pick(slot_ids // lanes, blocks * capacity // lanes)
    slot_low = pick(slot_ids % lanes, lanes)
    payload = jnp.stack([jnp.where(active, fe_traction[0], 0.0), (node_ids + 1).astype(jnp.float32)])
    outbox = jnp.einsum("pi,ia,ib->pab", payload, slot_high, slot_low, precision=highest)
    slip_new = slip + STEP_DT * rate
    wave_upper, wave_lower = table_halves(dip_table(blocks, groups, total_dip))
    lines = lax.all_to_all(slip_new, "dip", split_axis=0, concat_axis=1, tiled=True)

    residue = reverse_bits(strike_pos, levels)
    gain = 0.5 * SHEAR_MOD * scaling
    at = jnp.stack([residue, dip_pos * cols_here]).astype(jnp.int32)
    memory = weighted_history(history, at, blocks, total_strike, total_dip, gain)
    memory = memory.reshape(2 * rows_here, cols_here)

    turn_cos, turn_sin = twiddles(blocks, rows_here)
    memory = jnp.einsum("qk,qm->km", memory, line_table(rows_here, 1.0), precision=high)
    here_cos = lax.dynamic_slice_in_dim(jnp.asarray(turn_cos), residue, 1, 0)
    here_sin = lax.dynamic_slice_in_dim(jnp.asarray(turn_sin), residue, 1, 0)
    mem_re, mem_im = memory[:, :rows_here], memory[:, rows_here:]
    memory = jnp.concatenate(
        [mem_re * here_cos - mem_im * here_sin, mem_im * here_cos + mem_re * here_sin], axis=1
    )
    sign = jnp.where(lax.broadcasted_iota(jnp.int32, (1, 2 * rows_here), 1) < rows_here, 1.0, -1.0)
    opposite = [rev[(blocks - rev[s]) % blocks] for s in range(blocks)]
    lower_side = dip_pos < groups // 2
    first_row = memory[:1]
    other = lax.ppermute(
        first_row,
        both,
        [(s * groups + d, opposite[s] * groups + d) for s in range(blocks) for d in range(groups)],
    )
    place = lax.broadcasted_iota(jnp.int32, (cols_here, cols_here), 0)
    place = jnp.where(lower_side, place, (cols_here - place) % cols_here)
    turned = (place == lax.broadcasted_iota(jnp.int32, (cols_here, cols_here), 1)).astype(
        jnp.bfloat16
    )
    mem_upper, mem_lower = halves(memory)
    memory = dot_f32("ak,km->am", turned, jnp.concatenate([mem_upper, mem_lower], axis=1))
    memory = memory[:, : 2 * rows_here] + memory[:, 2 * rows_here :]
    keep = jnp.where(lower_side, memory[:half_cols], memory[half_cols:])
    give = jnp.where(lower_side, memory[half_cols:], memory[:half_cols])
    lines, keep, give = lax.optimization_barrier((lines, keep, give))
    given = lax.ppermute(
        give,
        both,
        [
            (s * groups + d, opposite[s] * groups + groups - 1 - d)
            for s in range(blocks)
            for d in range(groups)
        ],
    )

    lines_upper, lines_lower = halves(lines)
    modes = dot_f32("kc,rc->kr", wave_upper, jnp.concatenate([lines_upper, lines_lower], axis=0))
    modes = modes[:, :rows_line] + modes[:, rows_line:]
    modes = modes + dot_f32("kc,rc->kr", wave_lower, lines_upper)
    modes = modes.reshape(devices, 2 * per_device, rows_line)
    modes = lax.all_to_all(modes, both, split_axis=0, concat_axis=0, tiled=True)

    own_mirror = (dip_pos == 0) | (dip_pos == groups // 2)
    first_row = jnp.where(own_mirror, 0.5 * (first_row + sign * other), first_row)
    edge_row = lax.ppermute(
        first_row,
        both,
        [
            (s * groups + d, opposite[s] * groups + (groups - d) % (groups // 2))
            for s in range(blocks)
            for d in range(groups // 2, groups)
        ],
    )
    folded = jnp.where(lower_side, keep, given) + sign * jnp.where(lower_side, given, keep)
    packed = jnp.concatenate(
        [
            first_row[:, :rows_here] + edge_row[:, rows_here:],
            first_row[:, rows_here:] + edge_row[:, :rows_here],
        ],
        axis=1,
    )
    edge = jnp.where(dip_pos == 0, packed, first_row + sign * edge_row)
    at_first = lax.broadcasted_iota(jnp.int32, (half_cols, 1), 0) == 0
    folded = jnp.where(at_first & lower_side, edge, folded)
    width = 2 * rows_here
    sent_rows = 2 * capacity // width
    outbox = jnp.swapaxes(outbox.reshape(2, blocks, capacity), 0, 1)
    folded = folded.reshape(blocks, per_device, width)
    folded = jnp.concatenate([folded, outbox.reshape(blocks, sent_rows, width)], axis=1)
    modes, folded = lax.optimization_barrier((modes, folded))
    folded = lax.all_to_all(folded, "strike", split_axis=0, concat_axis=0, tiled=True)
    memory = folded[:, :per_device]
    received = jnp.swapaxes(folded[:, per_device:].reshape(blocks, 2, capacity), 0, 1)
    chunk = min(256, blocks * capacity)
    nodes = (received[1] + 0.5).reshape(-1, 1, chunk)
    used = (jnp.max(nodes, axis=(1, 2)) >= 1.0).astype(jnp.int32)
    traction = scatter_rows(used, nodes, received[0].reshape(-1, 1, chunk), rows_here, cols_here)

    modes = jnp.swapaxes(modes, 0, 1).reshape(2, per_device, blocks, rows_here)
    line_re = jnp.concatenate([modes[0], modes[0, :1]], axis=0)
    line_im = jnp.concatenate([modes[1], -modes[1, :1]], axis=0)
    line_re, line_im = block_transform(line_re, line_im, -1.0)
    line_re, line_im = (
        line_re * turn_cos + line_im * turn_sin,
        line_im * turn_cos - line_re * turn_sin,
    )
    spec = jnp.concatenate([line_re, line_im], axis=-1)
    spec = jnp.einsum("krm,mq->krq", spec, line_table(rows_here, -1.0), precision=high)

    turn_at = jnp.where(dip_pos < groups // 2, 2 * dip_pos, 2 * (groups - 1 - dip_pos) + 1)
    first_mode = turn_at * half_cols + strike_pos * per_device
    dims = (per_device, blocks, rows_here)
    mode_at = first_mode + lax.broadcasted_iota(jnp.int32, dims, 0)
    freq_row = lax.broadcasted_iota(jnp.int32, dims, 1) + blocks * lax.broadcasted_iota(
        jnp.int32, dims, 2
    )
    factor = -0.5 * SHEAR_MOD * scaling * scaling
    filt = 2.0 * factor * wavenumber(freq_row, mode_at, total_strike, total_dip)
    filt = jnp.concatenate([filt, filt], axis=-1)
    is_first = first_mode == 0
    edge_row = freq_row[:1]
    edge_low = factor * wavenumber(edge_row, edge_row * 0, total_strike, total_dip)
    edge_top = factor * wavenumber(
        edge_row, edge_row * 0 + total_dip // 2, total_strike, total_dip
    )
    edge_low = jnp.concatenate([edge_low, edge_low], axis=-1)
    edge_top = jnp.concatenate([edge_top, edge_top], axis=-1)
    direct, mirror = spec[:1], spec[per_device:]
    edge = 0.5 * (edge_low * (direct + mirror) + edge_top * (direct - mirror))
    spec = spec[:per_device] * filt
    spec = jnp.concatenate([jnp.where(is_first, edge, spec[:1]), spec[1:]], axis=0)
    spec = jnp.einsum("krq,qm->krm", spec, line_table(rows_here, 1.0), precision=high)
    back_re, back_im = spec[..., :rows_here], spec[..., rows_here:]
    back_re, back_im = (
        back_re * turn_cos - back_im * turn_sin,
        back_im * turn_cos + back_re * turn_sin,
    )

    back_re, back_im, memory = lax.optimization_barrier((back_re, back_im, memory))
    parts = []
    for r in range(blocks):
        o = (blocks - r) % blocks
        parts.append(jnp.where(lower_side, memory[rev[r]], memory[rev[o]]))
    back_re = back_re + jnp.stack([part[:, :rows_here] for part in parts], axis=1)
    back_im = back_im + jnp.stack([part[:, rows_here:] for part in parts], axis=1)

    back_re, back_im = block_transform(back_re, back_im, 1.0)
    back = jnp.stack([back_re, back_im]).reshape(2 * per_device, devices, rows_line)
    back = lax.all_to_all(
        jnp.swapaxes(back, 0, 1), both, split_axis=0, concat_axis=0, tiled=True
    )
    back, traction = lax.optimization_barrier((back, traction))
    back = back.reshape(total_dip, rows_line)
    back_upper, back_lower = halves(back)
    functional = dot_f32("kr,kc->rc", jnp.concatenate([back_upper, back_lower], axis=1), wave_upper)
    functional = functional[:rows_line] + functional[rows_line:]
    functional = functional + dot_f32("kr,kc->rc", back_upper, wave_lower)
    functional = lax.all_to_all(functional, "dip", split_axis=1, concat_axis=0, tiled=True)

    stress = prestress + functional + traction
    strength = normal_stress * (STATIC_FR - (STATIC_FR - DYNAMIC_FR) * jnp.minimum(slip_new, 1.0))
    new_rate = jnp.where(fric_flag == 1, jnp.maximum(stress - strength, 0.0) / DAMPING, 0.0)
    sampled = gather_rows(used, nodes, new_rate).reshape(blocks, capacity)
    returned = lax.all_to_all(sampled, "strike", split_axis=0, concat_axis=0, tiled=True)
    returned = jnp.einsum(
        "ia,ab->ib", slot_high, returned.reshape(-1, lanes), precision=highest
    )
    fe_rate = jnp.where(active, jnp.sum(returned * slot_low, axis=1), 0.0)
    return (new_rate, stress, fe_rate[None])


def solution(mesh):
    in_specs = (
        P("strike", "dip"),
        P("strike", "dip"),
        P("strike", "dip"),
        P("strike", "dip"),
        P(None, None, "strike", "dip"),
        P("strike", "dip"),
        P("dip", "strike", None),
        P("dip", "strike"),
        P("dip", "strike"),
        P("dip", "strike"),
    )
    out_specs = (P("strike", "dip"), P("strike", "dip"), P("dip", "strike"))
    return jax.shard_map(body, mesh=mesh, in_specs=in_specs, out_specs=out_specs, check_vma=False)
```
